128 devices in a mesh: dp: 4 (over y), expert: 32 (over x, z, core).
Axes of the slice: x: 4, y: 4, z: 4, core: 2. Of those that a mesh axis runs over, the one named last changes fastest.
Arguments:
- tokens: bfloat16 [262144, 3584], P(('dp', 'expert'))
- grads_out: bfloat16 [262144, 1024], P(('dp', 'expert')), may hold values from -0.0625 to 0.0625
- counts: int32 [128, 2], P(('dp', 'expert')), may hold values from 1 to 1920, as said below
- placement: int32 [32], replicated, may hold values from 0 to 31, as said below
- limits: float32 [32], P('expert'), may hold values from 0.3 to 1.5
Outputs:
- clipped: bfloat16 [32, 3584, 1024], P('expert', 'dp')
The draws below stay inside these ranges and needn't reach their ends.
Inputs may be any that keep to these rules, and one draw needn't show every extreme that they name: For every device, the two counts rounded up to multiples of 128 sum to exactly 2048. Expert c's own slot is on expert index c; the redundant slot on expert index e copies expert placement[e]. An expert may have several copies or none.
All inputs are finite; a program needn't handle non-finite values.
Results may differ from the reference program's by a relative error of at most 0.015.
Values may be sent and summed in bfloat16 or wider, within the bound.
A program may use at most 128 MiB of HBM per device.

```python
import math
import jax
import jax.numpy as jnp
from jax import lax

DW = 3584
FW = 1024
BLOCK = 128
BLOCKS_DEV = 16
ROWS = 2048
ALL_ROWS = 262144
EXPERTS = 32
N_DP = 4
N_EXPERT = 32


def draw_tokens(key, part):
    key = jax.random.fold_in(key, 11)
    key_cols, key_vals = jax.random.split(key)
    trend = jnp.exp(jnp.linspace(-0.55, 0.55, DW, dtype=jnp.float32))
    column_scale = trend * jnp.exp(jax.random.uniform(key_cols, (DW,), jnp.float32, -0.7, 0.7))
    values = jax.random.normal(key_vals, (ALL_ROWS, DW), jnp.float32)
    return (values * column_scale[None, :]).astype(jnp.bfloat16)


def draw_counts(key, part):
    key = jax.random.fold_in(key, 23)
    key_a, key_b, key_c, key_d = jax.random.split(key, 4)
    device_count = N_DP * N_EXPERT
    first_blocks = jax.random.randint(key_a, (device_count,), 1, BLOCKS_DEV)
    first_tail = jax.random.randint(key_b, (device_count,), 1, BLOCK + 1)
    second_tail = jax.random.randint(key_c, (device_count,), 1, BLOCK + 1)
    chosen = jax.random.randint(key_d, (), 0, device_count)
    marked = jnp.arange(device_count) == chosen
    first_blocks = jnp.where(marked, BLOCKS_DEV - 1, first_blocks)
    first_tail = jnp.where(marked, BLOCK, first_tail)
    second_blocks = BLOCKS_DEV - first_blocks
    first_count = BLOCK * (first_blocks - 1) + first_tail
    second_count = BLOCK * (second_blocks - 1) + second_tail
    return jnp.stack([first_count, second_count], axis=1).astype(jnp.int32)


def draw_placement(key, part):
    key = jax.random.fold_in(key, 37)
    key_a, key_b, key_c = jax.random.split(key, 3)
    order = jax.random.permutation(key_a, N_EXPERT)
    popular = jax.random.randint(key_b, (N_EXPERT,), 0, max(N_EXPERT // 4, 2))
    chosen = order[popular]
    spots = jax.random.permutation(key_c, N_EXPERT)
    chosen = chosen.at[spots[0]].set(0)
    chosen = chosen.at[spots[1]].set(N_EXPERT - 1)
    return chosen.astype(jnp.int32)


def levels(rng, extent, pieces, least, top_value):
    loudness = 1.0
    for dim, shards_of in pieces:
        heights = jax.random.uniform(jax.random.fold_in(jax.random.fold_in(rng, 6), dim), (shards_of,), jnp.float32, least / len(pieces), top_value / len(pieces))
        loudness = loudness * jnp.repeat(jnp.exp(heights), extent[dim] // shards_of).reshape((-1,) + (1,) * (len(extent) - 1 - dim))
    return loudness


def noise(own_key, extent, spread, bound, cuts=(), kind=jnp.bfloat16):
    array = jax.random.normal(own_key, extent, jnp.float32) * spread
    if len(cuts) > 0:
        array = levels(own_key, extent, cuts, -0.22, 0.18) * array
    return jnp.clip(array, min=-bound, max=bound).astype(kind)


def setup_inputs(seed: int = 0) -> dict:
    seeds = jax.random.split(jax.random.key(seed), 6)
    return {
        "tokens": draw_tokens(jax.random.fold_in(seeds[5], 71), 0),
        "grads_out": noise(seeds[1], (ALL_ROWS, FW), (N_DP * ROWS) ** -0.5, 0.0625, ((0, 128),)),
        "counts": draw_counts(jax.random.fold_in(seeds[5], 71), 0),
        "placement": draw_placement(jax.random.fold_in(seeds[5], 71), 0),
        "limits": jnp.clip(jnp.exp(math.log(1.5) - 1.60943787 * jax.random.uniform(seeds[4], (EXPERTS,), jnp.float32) ** levels(seeds[4], (EXPERTS,), ((0, 32),), -0.2, 0.2)), 0.3, 1.5),
    }


def reference(tokens, grads_out, counts, placement, limits):
    device_count = N_DP * N_EXPERT
    token_blocks = tokens.reshape(device_count, ROWS, DW)
    grad_blocks = grads_out.reshape(device_count, ROWS, FW)
    position = jnp.arange(ROWS, dtype=jnp.int32)
    contract = (((0,), (0,)), ((), ()))

    def visit(total, inputs):
        token_rows, grad_rows, count_pair, device = inputs
        expert_slot = device % N_EXPERT
        first_count = count_pair[0]
        second_count = count_pair[1]
        padded_first = (first_count + BLOCK - 1) // BLOCK * BLOCK
        keep_first = (position < first_count).astype(grad_rows.dtype)[:, None]
        keep_second = ((position >= padded_first) & (position < padded_first + second_count)).astype(grad_rows.dtype)[:, None]
        first_part = lax.dot_general(token_rows, grad_rows * keep_first, contract, preferred_element_type=jnp.float32)
        second_part = lax.dot_general(token_rows, grad_rows * keep_second, contract, preferred_element_type=jnp.float32)
        first_part = lax.optimization_barrier(first_part.astype(jnp.bfloat16)).astype(jnp.float32)
        second_part = lax.optimization_barrier(second_part.astype(jnp.bfloat16)).astype(jnp.float32)
        total = total.at[expert_slot].add(first_part)
        total = total.at[placement[expert_slot]].add(second_part)
        return (total, None)
    start = jnp.zeros((EXPERTS, DW, FW), jnp.float32)
    devices = jnp.arange(device_count, dtype=jnp.int32)
    total, _ = lax.scan(visit, start, (token_blocks, grad_blocks, counts, devices))
    square_sum = lax.optimization_barrier(jnp.sum(total * total, axis=(1, 2)))
    threshold = limits * jnp.sqrt(jnp.float32(DW * FW))
    factor = jnp.minimum(1.0, threshold / jnp.sqrt(square_sum + 1e-06))
    return (total * factor[:, None, None]).astype(jnp.bfloat16)
```

```python
import functools
import math

import jax
import jax.numpy as jnp
from jax import lax
from jax.experimental import pallas as pl
from jax.experimental.pallas import tpu as pltpu
from jax.sharding import PartitionSpec as P

MESH = pl.DeviceIdType.MESH
BF = jnp.bfloat16
F32 = jnp.float32

DP = 4
EX = 32
ROWS = 2048
DW = 3584
FW = 1024
HW = FW // 2
CH = 128
NJ = DW // DP // CH
ND = 2
NA = NJ - ND
NU = 2 * NA + ND
NX = 3

FIRST = [(0, 1), (1, 1), (NA, 1), (2, 1), (NA + 1, 1), (3, 1), (4, 1)]
SECOND = [(j, 0) for j in range(NJ)]


def unit(j, s):
    return j if s == 1 else NA + j


def body(
    x_ref, g_ref, counts_ref, place_ref, limit_ref, out_ref, factor_ref,
    xc, G, Pb, H1, H2, d_in, d_mid, d_back, S1, a_in, a_mid, a_back, CD, CA,
    T, acc, norms, tab_v, tab_s,
    x_sem, g_sem, tab_sem, y_send, h1_sem, h2_sem, a2a_send, a2a_recv, own_sem,
    n_send, n_recv, out_sem,
):
    d = lax.axis_index("dp")
    e = lax.axis_index("expert")
    up = lax.rem(d + 1, DP)
    dn = lax.rem(d + 3, DP)
    opp = lax.rem(d + 2, DP)
    ex = e // 8
    ez = lax.rem(e // 2, 4)
    ec = lax.rem(e, 2)
    turn = 1 - 2 * ec

    def peer(i):
        px = lax.rem(ex + turn * (i // 8) + 4, 4)
        pz = lax.rem(ez + turn * lax.rem(i // 2, 4) + 4, 4)
        pc = lax.rem(ec + lax.rem(i, 2), 2)
        return (px * 4 + pz) * 2 + pc

    def g_load(s):
        return pltpu.make_async_copy(g_ref, G.at[:, pl.ds(s * FW, FW)], g_sem.at[s])

    def x_load(i, j):
        return [
            pltpu.make_async_copy(
                x_ref.at[:, pl.ds(t * (DW // DP) + j * CH, CH)],
                xc.at[i % NX, :, pl.ds(t * CH, CH)],
                x_sem.at[(i % NX) * 4 + t],
            )
            for t in range(4)
        ]

    steps = FIRST + SECOND
    g_load(1).start()
    for i in range(NX - 1):
        for c in x_load(i, steps[i][0]):
            c.start()
    g_load(0).start()

    bar = pltpu.get_barrier_semaphore()
    for k in range(1, DP):
        pl.semaphore_signal(
            bar, inc=1, device_id=(lax.rem(d + k, DP), e), device_id_type=MESH
        )

    def greet(k, c):
        pl.semaphore_signal(
            bar, inc=1, device_id=(d, lax.rem(e + k, EX)), device_id_type=MESH
        )
        return c

    lax.fori_loop(1, EX, greet, 0)

    row = place_ref[...]
    ri = lax.broadcasted_iota(jnp.int32, (EX, EX), 0)
    ci = lax.broadcasted_iota(jnp.int32, (EX, EX), 1)
    across = jnp.broadcast_to(row, (EX, EX))
    down = jnp.sum(jnp.where(ri == ci, across, 0), axis=1, keepdims=True)
    tab_v[0:1, 0:EX] = jnp.max(
        jnp.where((down == across) & (ri < ci), ri + 1, 0), axis=0, keepdims=True
    )
    tab_v[1:2, 0:EX] = jnp.max(
        jnp.where(down == ci, ri + 1, 0), axis=0, keepdims=True
    )
    tab = pltpu.make_async_copy(tab_v, tab_s, tab_sem)
    tab.start()

    first = counts_ref[0, 0]
    second = counts_ref[0, 1]
    padded = (first + 127) // 128 * 128

    def mask(s):
        g_load(s).wait()
        lo = padded if s == 1 else 0
        hi = padded + second if s == 1 else first

        @pl.loop(0, ROWS // 128)
        def _(b):
            r = pl.ds(pl.multiple_of(b * 128, 128), 128)
            pos = lax.broadcasted_iota(jnp.int32, (128, FW), 0) + b * 128
            g = G[r, pl.ds(s * FW, FW)]
            G[r, pl.ds(s * FW, FW)] = jnp.where(
                (pos >= lo) & (pos < hi), g, jnp.zeros_like(g)
            )

    state = {"i": 0}

    def compute(j, s):
        i = state["i"]
        state["i"] = i + 1
        assert steps[i] == (j, s)
        n = i + NX - 1
        if n < len(steps):
            for c in x_load(n, steps[n][0]):
                c.start()
        for c in x_load(i, j):
            c.wait()

        @pl.loop(0, FW // 512)
        def _(n):
            col = pl.ds(pl.multiple_of(s * FW + n * 512, 512), 512)
            r = lax.dot_general(
                xc[i % NX],
                G[:, col],
                (((0,), (0,)), ((), ())),
                preferred_element_type=F32,
            )
            Pb[j, :, :, col] = r.astype(BF).reshape(4, CH, 512)

    def y_copy(src, dst, u, sem, target):
        return pltpu.make_async_remote_copy(
            src, dst, y_send.at[u], sem, device_id=(target, e), device_id_type=MESH
        )

    def halves(s):
        return pl.ds(s * FW, HW), pl.ds(s * FW + HW, HW)

    left, right = pl.ds(0, HW), pl.ds(HW, HW)

    def raw(j, s):
        u = unit(j, s)
        ha, hb = halves(s)
        y_copy(Pb.at[j, opp, :, ha], H1.at[0, u], u, h1_sem.at[0, u], dn).start()
        y_copy(Pb.at[j, opp, :, hb], H1.at[1, u], u, h1_sem.at[1, u], up).start()
        y_copy(Pb.at[j, dn, :, hb], H2.at[0, u, :, right], u, h2_sem.at[0, u], dn).start()
        y_copy(Pb.at[j, up, :, ha], H2.at[1, u, :, left], u, h2_sem.at[1, u], up).start()

    def merge(j, s):
        u = unit(j, s)
        ha, hb = halves(s)
        for k, t, h, half in ((0, dn, ha, left), (1, up, hb, right)):
            pltpu.make_async_copy(H1.at[k, u], H1.at[k, u], h1_sem.at[k, u]).wait()

            @pl.loop(0, CH // 32)
            def _(b):
                r = pl.ds(pl.multiple_of(b * 32, 32), 32)
                v = Pb[j, t, r, h].astype(F32) + H1[k, u, r, :].astype(F32)
                Pb[j, t, r, h] = v.astype(BF)

            y_copy(
                Pb.at[j, t, :, h], H2.at[k, u, :, half], u, h2_sem.at[k, u], t
            ).start()

    def arrived(u):
        for k in range(2):
            pltpu.make_async_copy(H2.at[k, u], H2.at[k, u], h2_sem.at[k, u]).wait()

    def reduce_second(j):
        u = unit(j, 1)
        arrived(u)

        @pl.loop(0, CH // 16)
        def _(b):
            r = pl.ds(pl.multiple_of(b * 16, 16), 16)
            v = Pb[j, d, r, pl.ds(FW, FW)].astype(F32)
            v = v + H2[0, u, r, :].astype(F32) + H2[1, u, r, :].astype(F32)
            S1[j, r, :] = v.astype(BF)

    def exchange(a, src, dst):
        own = pltpu.make_async_copy(src(e), dst.at[e], own_sem.at[a])
        own.start()

        def send(i, c):
            p = peer(i)
            pltpu.make_async_remote_copy(
                src(p), dst.at[e], a2a_send.at[a], a2a_recv.at[a],
                device_id=(d, p), device_id_type=MESH,
            ).start()
            return c

        lax.fori_loop(1, EX, send, 0)
        return own

    def all_in(a, dst):
        pltpu.make_async_copy(
            dst.at[pl.ds(0, EX - 1)], dst.at[pl.ds(0, EX - 1)], a2a_recv.at[a]
        ).wait()

    def chain(inp, mid, C):
        C[0] = jnp.zeros(C.shape[1:], F32)

        def add(i, c):
            C[i + 1] = C[tab_s[0, i]] + inp[i].astype(F32)
            return c

        lax.fori_loop(0, EX, add, 0)

        def pick(i, c):
            mid[i] = C[tab_s[1, i]].astype(BF)
            return c

        lax.fori_loop(0, EX, pick, 0)

    owns = {}

    def d_route(k):
        j = NA + k

        def src(q):
            r = pl.ds(pl.multiple_of(lax.rem(q, 8) * 16, 16), 16)
            return Pb.at[j, q // 8, r, pl.ds(FW, FW)]

        owns[2 * k] = exchange(2 * k, src, d_in.at[k])

    def d_return(k):
        owns[2 * k].wait()
        all_in(2 * k, d_in.at[k])
        chain(d_in.at[k], d_mid.at[k], CD)
        owns[2 * k + 1] = exchange(2 * k + 1, lambda q: d_mid.at[k, q], d_back.at[k])

    def d_add(k):
        owns[2 * k + 1].wait()
        all_in(2 * k + 1, d_back.at[k])

        @pl.loop(0, EX)
        def _(q):
            t = q // 8
            r = pl.ds(pl.multiple_of(lax.rem(q, 8) * 16, 16), 16)
            v = Pb[NA + k, t, r, pl.ds(0, FW)].astype(F32) + d_back[k, q].astype(F32)
            Pb[NA + k, t, r, pl.ds(0, FW)] = v.astype(BF)

    A1, A2 = 2 * ND, 2 * ND + 1

    def a_route():
        def src(q):
            r = pl.ds(pl.multiple_of(q // 4 * 16, 16), 16)
            c = pl.ds(pl.multiple_of(lax.rem(q, 4) * 256, 256), 256)
            return S1.at[:, r, c]

        owns[A1] = exchange(A1, src, a_in)

    def a_return():
        owns[A1].wait()
        all_in(A1, a_in)
        chain(a_in, a_mid, CA)
        owns[A2] = exchange(A2, lambda q: a_mid.at[q], a_back)

    def a_ready():
        owns[A2].wait()
        all_in(A2, a_back)

    def total(j):
        u = unit(j, 0)
        arrived(u)

        @pl.loop(0, CH // 16)
        def _(b):
            r = pl.ds(pl.multiple_of(b * 16, 16), 16)
            for c in range(4):
                col = pl.ds(c * 256, 256)
                v = Pb[j, d, r, col].astype(F32)
                v = v + H2[0, u, r, col].astype(F32) + H2[1, u, r, col].astype(F32)
                if j < NA:
                    v = v + a_back[b * 4 + c, j].astype(F32)
                w = v * v
                acc[:, col] += w[0:8] + w[8:16]
                T[j, r, col] = v.astype(BF)

        out_copy(j).start()

    def out_copy(j):
        return pltpu.make_async_copy(
            T.at[j], out_ref.at[pl.ds(j * CH, CH), :], out_sem.at[j]
        )

    acc[...] = jnp.zeros_like(acc)
    mask(1)
    compute(0, 1)
    pl.semaphore_wait(bar, EX - 1 + DP - 1)
    raw(0, 1)
    compute(1, 1)
    raw(1, 1)
    compute(NA, 1)
    d_route(0)
    merge(0, 1)
    compute(2, 1)
    raw(2, 1)
    compute(NA + 1, 1)
    d_route(1)
    merge(1, 1)
    compute(3, 1)
    raw(3, 1)
    tab.wait()
    mask(0)
    merge(2, 1)
    compute(4, 1)
    raw(4, 1)
    d_return(0)
    merge(3, 1)
    compute(0, 0)
    compute(1, 0)
    merge(4, 1)
    raw(0, 0)
    raw(1, 0)
    d_return(1)
    compute(2, 0)
    raw(2, 0)
    merge(0, 0)
    compute(3, 0)
    raw(3, 0)
    compute(4, 0)
    for j in range(NA):
        reduce_second(j)
    a_route()
    raw(4, 0)
    compute(NA, 0)
    compute(NA + 1, 0)
    merge(1, 0)
    d_add(0)
    raw(NA, 0)
    merge(2, 0)
    d_add(1)
    raw(NA + 1, 0)
    merge(3, 0)
    a_return()
    merge(4, 0)
    merge(NA, 0)
    merge(NA + 1, 0)
    a_ready()
    for j in range(NJ):
        total(j)

    square = jnp.sum(acc[...])
    norms[d] = jnp.full((8, 128), square, F32)
    for k in range(1, DP):
        pltpu.make_async_remote_copy(
            norms.at[d], norms.at[d], n_send, n_recv,
            device_id=(lax.rem(d + k, DP), e), device_id_type=MESH,
        ).start()
    pltpu.make_async_copy(norms.at[pl.ds(0, 3)], norms.at[pl.ds(0, 3)], n_recv).wait()
    whole = norms[0] + norms[1] + norms[2] + norms[3]
    threshold = limit_ref[0] * math.sqrt(DW * FW)
    factor_ref[...] = jnp.minimum(1.0, threshold / jnp.sqrt(whole + 1e-06))

    pltpu.make_async_copy(norms.at[pl.ds(0, 3)], norms.at[pl.ds(0, 3)], n_send).wait()
    for u in range(NU):
        pltpu.make_async_copy(
            H2.at[0, pl.ds(0, 3)], H2.at[0, pl.ds(0, 3)], y_send.at[u]
        ).wait()
    for a in range(2 * ND + 2):
        ref = d_in.at[0] if a < 2 * ND else a_in
        pltpu.make_async_copy(
            ref.at[pl.ds(0, EX - 1)], ref.at[pl.ds(0, EX - 1)], a2a_send.at[a]
        ).wait()
    for j in range(NJ):
        out_copy(j).wait()


def local(tokens, grads_out, counts, placement, limits):
    dma = pltpu.SemaphoreType.DMA
    total, factor = pl.pallas_call(
        body,
        out_shape=(
            jax.ShapeDtypeStruct((DW // DP, FW), BF),
            jax.ShapeDtypeStruct((8, 128), F32),
        ),
        in_specs=[
            pl.BlockSpec(memory_space=pl.ANY),
            pl.BlockSpec(memory_space=pl.ANY),
            pl.BlockSpec(memory_space=pltpu.SMEM),
            pl.BlockSpec(memory_space=pltpu.VMEM),
            pl.BlockSpec(memory_space=pltpu.SMEM),
        ],
        out_specs=(
            pl.BlockSpec(memory_space=pl.ANY),
            pl.BlockSpec(memory_space=pltpu.VMEM),
        ),
        scratch_shapes=[
            pltpu.VMEM((NX, ROWS, 4 * CH), BF),
            pltpu.VMEM((ROWS, 2 * FW), BF),
            pltpu.VMEM((NJ, 4, CH, 2 * FW), BF),
            pltpu.VMEM((2, NU, CH, HW), BF),
            pltpu.VMEM((2, NU, CH, FW), BF),
            pltpu.VMEM((ND, EX, 16, FW), BF),
            pltpu.VMEM((ND, EX, 16, FW), BF),
            pltpu.VMEM((ND, EX, 16, FW), BF),
            pltpu.VMEM((NA, CH, FW), BF),
            pltpu.VMEM((EX, NA, 16, 256), BF),
            pltpu.VMEM((EX, NA, 16, 256), BF),
            pltpu.VMEM((EX, NA, 16, 256), BF),
            pltpu.VMEM((EX + 1, 16, FW), F32),
            pltpu.VMEM((EX + 1, NA, 16, 256), F32),
            pltpu.VMEM((NJ, CH, FW), BF),
            pltpu.VMEM((8, FW), F32),
            pltpu.VMEM((DP, 8, 128), F32),
            pltpu.VMEM((8, 128), jnp.int32),
            pltpu.SMEM((8, 128), jnp.int32),
            dma((NX * 4,)),
            dma((2,)),
            dma,
            dma((NU,)),
            dma((2, NU)),
            dma((2, NU)),
            dma((2 * ND + 2,)),
            dma((2 * ND + 2,)),
            dma((2 * ND + 2,)),
            dma,
            dma,
            dma((NJ,)),
        ],
        compiler_params=pltpu.CompilerParams(
            collective_id=0, has_side_effects=True, vmem_limit_bytes=62 * 2**20
        ),
        cost_estimate=pl.CostEstimate(
            flops=4 * ROWS * DW * FW, bytes_accessed=40 * 2**20, transcendentals=0
        ),
    )(tokens, grads_out, counts, placement.reshape(1, EX), limits)
    return (total.astype(F32) * factor[0, 0]).astype(BF)[None]


def solution(mesh):
    in_specs = (
        P(("dp", "expert"), None),
        P(("dp", "expert"), None),
        P(("dp", "expert"), None),
        P(),
        P("expert"),
    )
    out_specs = P("expert", "dp", None)
    return jax.shard_map(local, mesh=mesh, in_specs=in_specs, out_specs=out_specs, check_vma=False)
```

```python
import functools
import math

import jax
import jax.numpy as jnp
from jax import lax
from jax.experimental import pallas as pl
from jax.experimental.pallas import tpu as pltpu
from jax.sharding import PartitionSpec as P

MESH = pl.DeviceIdType.MESH
BF = jnp.bfloat16
F32 = jnp.float32

DP = 4
EX = 32
ROWS = 2048
DW = 3584
FW = 1024
HW = FW // 2
CH = 128
NJ = DW // DP // CH
ND = 3
NA = NJ - ND
NU = 2 * NA + ND
NG = NA // 2
NX = 3
PARTS = 4

START = ["c41", "c01"]
ORDER = [
    "c21", "w21", "h21", "c51", "dr1", "m01", "c11", "h11", "c31", "w31",
    "h31", "c00", "w00", "dret0", "h00", "m21", "c61", "m31", "c40", "dr2",
    "m00", "c30", "r0", "w11", "c10", "h10", "c20", "h20", "da0", "r3",
    "r2", "m11", "dret1", "h30", "w10", "w20", "h40", "c50", "m10", "c60",
    "dret2", "m30", "r1", "w30", "pre1", "m40", "ar0", "da1", "h50", "da2",
    "w50", "h60", "m20", "pre0", "ar1", "w60", "pre3", "aret0", "m60",
    "w40", "aret1", "m50", "ardy0", "tot4", "tot6", "pre2", "fin0", "fin1",
    "ardy1", "fin2", "fin3", "tot5",
]
STEPS = [(int(o[1]), int(o[2])) for o in START + ORDER if o[0] == "c"]


def unit(j, s):
    return j if s == 1 else NA + j


def body(
    x_ref, g_ref, counts_ref, place_ref, limit_ref, out_ref, norm_ref,
    xc, G, Pb, H1, H2, d_in, d_mid, d_back, S1, a_in, a_mid, a_back, CD, CA,
    T, acc, norm, tab_v, tab_s,
    z_sem, c_sem, x_sem, g_sem, tab_sem, y_send, h1_sem, h2_sem, a2a_send, a2a_recv, own_sem,
    n_send, n_recv, n_own, out_sem,
):
    d = lax.axis_index("dp")
    e = lax.axis_index("expert")
    up = lax.rem(d + 1, DP)
    dn = lax.rem(d + 3, DP)
    opp = lax.rem(d + 2, DP)
    ex = e // 8
    ez = lax.rem(e // 2, 4)
    ec = lax.rem(e, 2)
    turn = 1 - 2 * ec

    def peer(i):
        px = lax.rem(ex + turn * (i // 8) + 4, 4)
        pz = lax.rem(ez + turn * lax.rem(i, 4) + 4, 4)
        pc = lax.rem(ec + lax.rem(i // 4, 2), 2)
        return (px * 4 + pz) * 2 + pc

    def g_load(s, q):
        r = pl.ds(q * 512, 512)
        return pltpu.make_async_copy(
            g_ref.at[r, :], G.at[r, pl.ds(s * FW, FW)], g_sem.at[s * 4 + q]
        )

    def x_load(i, j):
        return [
            pltpu.make_async_copy(
                x_ref.at[:, pl.ds(t * (DW // DP) + j * CH, CH)],
                xc.at[i % NX, :, pl.ds(t * CH, CH)],
                x_sem.at[(i % NX) * 4 + t],
            )
            for t in range(4)
        ]

    steps = STEPS
    for q in range(4):
        g_load(1, q).start()
    for i in range(NX - 1):
        for c in x_load(i, steps[i][0]):
            c.start()
    for q in range(4):
        g_load(0, q).start()

    def at(kx, kz, kc):
        return (lax.rem(ex + kx, 4) * 4 + lax.rem(ez + kz, 4)) * 2 + lax.rem(ec + kc, 2)

    def signal(sem, td, te):
        pl.semaphore_signal(sem, inc=1, device_id=(td, te), device_id_type=MESH)

    bar = pltpu.get_barrier_semaphore()
    for k in range(1, 4):
        signal(bar, lax.rem(d + k, DP), e)
        signal(bar, d, at(k, 0, 0))
        signal(bar, d, at(0, k, 0))
    signal(bar, d, at(0, 0, 1))

    def greet_near():
        pl.semaphore_wait(bar, 10)
        for k in range(1, 4):
            signal(z_sem, d, at(0, k, 0))

    def greet_plane():
        pl.semaphore_wait(z_sem, 3)
        signal(c_sem, d, at(0, 0, 1))

    def plane_ready():
        pl.semaphore_wait(c_sem, 1)

    row = place_ref[...]
    ri = lax.broadcasted_iota(jnp.int32, (EX, EX), 0)
    ci = lax.broadcasted_iota(jnp.int32, (EX, EX), 1)
    across = jnp.broadcast_to(row, (EX, EX))
    down = jnp.sum(jnp.where(ri == ci, across, 0), axis=1, keepdims=True)
    tab_v[0:1, 0:EX] = jnp.max(
        jnp.where((down == across) & (ri < ci), ri + 1, 0), axis=0, keepdims=True
    )
    tab_v[1:2, 0:EX] = jnp.max(
        jnp.where(down == ci, ri + 1, 0), axis=0, keepdims=True
    )
    tab = pltpu.make_async_copy(tab_v, tab_s, tab_sem)
    tab.start()

    first = counts_ref[0, 0]
    second = counts_ref[0, 1]
    padded = (first + 127) // 128 * 128

    def mask(s):
        lo = padded if s == 1 else 0
        hi = padded + second if s == 1 else first
        for q in range(4):
            g_load(s, q).wait()

            @pl.loop(0, 4)
            def _(b):
                r = pl.ds(pl.multiple_of(q * 512 + b * 128, 128), 128)
                pos = lax.broadcasted_iota(jnp.int32, (128, FW), 0) + (q * 512 + b * 128)
                g = G[r, pl.ds(s * FW, FW)]
                G[r, pl.ds(s * FW, FW)] = jnp.where(
                    (pos >= lo) & (pos < hi), g, jnp.zeros_like(g)
                )

    def prefetch(n):
        if n < len(steps):
            for c in x_load(n, steps[n][0]):
                c.start()

    def half(i, n):
        j, s = steps[i]
        col = pl.ds(pl.multiple_of(s * FW + n * 512, 512), 512)
        r = lax.dot_general(
            xc[i % NX],
            G[:, col],
            (((0,), (0,)), ((), ())),
            preferred_element_type=F32,
        )
        Pb[j, :, :, col] = r.astype(BF).reshape(4, CH, 512)

    def x_wait(i):
        for c in x_load(i, steps[i][0]):
            c.wait()

    def compute(j, s):
        i = steps.index((j, s))
        prefetch(i + NX - 1)
        x_wait(i)
        pl.loop(0, 2)(functools.partial(half, i))

    def y_copy(src, dst, u, sem, target):
        return pltpu.make_async_remote_copy(
            src, dst, y_send.at[u], sem, device_id=(target, e), device_id_type=MESH
        )

    def halves(s):
        return pl.ds(s * FW, HW), pl.ds(s * FW + HW, HW)

    left, right = pl.ds(0, HW), pl.ds(HW, HW)

    def raw_left(j, s):
        u = unit(j, s)
        ha, hb = halves(s)
        y_copy(Pb.at[j, opp, :, ha], H1.at[0, u], u, h1_sem.at[0, u], dn).start()
        y_copy(Pb.at[j, up, :, ha], H2.at[1, u, :, left], u, h2_sem.at[1, u], up).start()

    def raw_right(j, s):
        u = unit(j, s)
        ha, hb = halves(s)
        y_copy(Pb.at[j, opp, :, hb], H1.at[1, u], u, h1_sem.at[1, u], up).start()
        y_copy(Pb.at[j, dn, :, hb], H2.at[0, u, :, right], u, h2_sem.at[0, u], dn).start()

    def first_hop(j, s):
        u = unit(j, s)
        ha, hb = halves(s)
        y_copy(Pb.at[j, opp, :, ha], H1.at[0, u], u, h1_sem.at[0, u], dn).start()
        y_copy(Pb.at[j, opp, :, hb], H1.at[1, u], u, h1_sem.at[1, u], up).start()

    def whole_hop(j, s):
        u = unit(j, s)
        ha, hb = halves(s)
        y_copy(Pb.at[j, dn, :, hb], H2.at[0, u, :, right], u, h2_sem.at[0, u], dn).start()
        y_copy(Pb.at[j, up, :, ha], H2.at[1, u, :, left], u, h2_sem.at[1, u], up).start()

    def merge(j, s):
        u = unit(j, s)
        ha, hb = halves(s)
        for k, t, h, half in ((0, dn, ha, left), (1, up, hb, right)):
            pltpu.make_async_copy(H1.at[k, u], H1.at[k, u], h1_sem.at[k, u]).wait()

            @pl.loop(0, CH // 32)
            def _(b):
                r = pl.ds(pl.multiple_of(b * 32, 32), 32)
                v = Pb[j, t, r, h].astype(F32) + H1[k, u, r, :].astype(F32)
                Pb[j, t, r, h] = v.astype(BF)

            y_copy(
                Pb.at[j, t, :, h], H2.at[k, u, :, half], u, h2_sem.at[k, u], t
            ).start()

    def arrived(u):
        for k in range(2):
            pltpu.make_async_copy(H2.at[k, u], H2.at[k, u], h2_sem.at[k, u]).wait()

    def reduce_second(j):
        u = unit(j, 1)
        arrived(u)

        @pl.loop(0, CH // 16)
        def _(b):
            r = pl.ds(pl.multiple_of(b * 16, 16), 16)
            v = Pb[j, d, r, pl.ds(FW, FW)].astype(F32)
            v = v + H2[0, u, r, :].astype(F32) + H2[1, u, r, :].astype(F32)
            S1[j, r, :] = v.astype(BF)

    def one(a, src, dst, p):
        pltpu.make_async_remote_copy(
            src(p), dst.at[e], a2a_send.at[a], a2a_recv.at[a],
            device_id=(d, p), device_id_type=MESH,
        ).start()

    def keep_own(a, src, dst):
        own = pltpu.make_async_copy(src(e), dst.at[e], own_sem.at[a])
        own.start()
        return own

    def exchange(a, src, dst):
        def send(i, c):
            one(a, src, dst, peer(i))
            return c

        lax.fori_loop(1, EX, send, 0)
        return keep_own(a, src, dst)

    def all_in(a, dst):
        pltpu.make_async_copy(
            dst.at[pl.ds(0, EX - 1)], dst.at[pl.ds(0, EX - 1)], a2a_recv.at[a]
        ).wait()

    def chain(inp, mid, C):
        C[0] = jnp.zeros(C.shape[1:], F32)

        def add(i, c):
            C[i + 1] = C[tab_s[0, i]] + inp[i].astype(F32)
            return c

        lax.fori_loop(0, EX, add, 0)

        def pick(i, c):
            mid[i] = C[tab_s[1, i]].astype(BF)
            return c

        lax.fori_loop(0, EX, pick, 0)

    owns = {}

    def d_src(k, q):
        r = pl.ds(pl.multiple_of(lax.rem(q, 8) * 16, 16), 16)
        return Pb.at[NA + k, q // 8, r, pl.ds(FW, FW)]

    def d_route(k):
        owns[2 * k] = exchange(2 * k, functools.partial(d_src, k), d_in.at[k])

    def d_return(k):
        owns[2 * k].wait()
        all_in(2 * k, d_in.at[k])
        chain(d_in.at[k], d_mid.at[k], CD)
        owns[2 * k + 1] = exchange(2 * k + 1, lambda q: d_mid.at[k, q], d_back.at[k])

    def d_add(k):
        owns[2 * k + 1].wait()
        all_in(2 * k + 1, d_back.at[k])

        @pl.loop(0, EX)
        def _(q):
            t = q // 8
            r = pl.ds(pl.multiple_of(lax.rem(q, 8) * 16, 16), 16)
            v = Pb[NA + k, t, r, pl.ds(0, FW)].astype(F32) + d_back[k, q].astype(F32)
            Pb[NA + k, t, r, pl.ds(0, FW)] = v.astype(BF)

    def a_route(g):
        def src(q):
            r = pl.ds(pl.multiple_of(q // 4 * 16, 16), 16)
            c = pl.ds(pl.multiple_of(lax.rem(q, 4) * 256, 256), 256)
            return S1.at[pl.ds(g * NG, NG), r, c]

        a = 2 * (ND + g)
        owns[a] = exchange(a, src, a_in.at[g])

    def a_return(g):
        a = 2 * (ND + g)
        owns[a].wait()
        all_in(a, a_in.at[g])
        chain(a_in.at[g], a_mid.at[g], CA)
        owns[a + 1] = exchange(a + 1, lambda q: a_mid.at[g, q], a_back.at[g])

    def a_ready(g):
        a = 2 * (ND + g) + 1
        owns[a].wait()
        all_in(a, a_back.at[g])

    def sums(j, b, col):
        u = unit(j, 0)
        r = pl.ds(pl.multiple_of(b * 16, 16), 16)
        v = Pb[j, d, r, col].astype(F32)
        return v + H2[0, u, r, col].astype(F32) + H2[1, u, r, col].astype(F32)

    def finish(j, b, col, v):
        w = v * v
        acc[:, col] += w[0:8] + w[8:16]
        T[j, pl.ds(pl.multiple_of(b * 16, 16), 16), col] = v.astype(BF)

    def pre(j):
        arrived(unit(j, 0))

        @pl.loop(0, CH // 16)
        def _(b):
            CD[j * 8 + b] = sums(j, b, pl.ds(0, FW))

    def fin(j):
        @pl.loop(0, CH // 16)
        def _(b):
            for c in range(4):
                col = pl.ds(c * 256, 256)
                v = CD[j * 8 + b, :, col] + a_back[j // NG, b * 4 + c, j % NG].astype(F32)
                finish(j, b, col, v)

        out_copy(j).start()

    def total(j):
        arrived(unit(j, 0))

        @pl.loop(0, CH // 16)
        def _(b):
            for c in range(4):
                col = pl.ds(c * 256, 256)
                finish(j, b, col, sums(j, b, col))

        out_copy(j).start()

    def out_copy(j):
        return pltpu.make_async_copy(
            T.at[j], out_ref.at[pl.ds(j * CH, CH), :], out_sem.at[j]
        )

    acc[...] = jnp.zeros_like(acc)
    mask(1)
    src0 = functools.partial(d_src, 0)
    route0 = functools.partial(one, 0, src0, d_in.at[0])
    prefetch(2)
    x_wait(0)
    pl.loop(0, 2)(functools.partial(half, 0))
    greet_near()
    for k in range(1, 4):
        route0(at(k, 0, 0))
        route0(at(0, k, 0))
    route0(at(0, 0, 1))
    prefetch(3)
    x_wait(1)
    half(1, 0)
    raw_left(0, 1)
    greet_plane()
    for k in range(1, 4):
        for m in range(1, 4):
            route0(at(k, m, 0))
        route0(at(0, k, 1))
    half(1, 1)
    raw_right(0, 1)
    plane_ready()
    for k in range(1, 4):
        for m in range(4):
            route0(at(k, m, 1))
    owns[0] = keep_own(0, src0, d_in.at[0])

    actions = {
        "c": compute, "h": first_hop, "w": whole_hop, "m": merge, "dr": d_route, "dret": d_return,
        "da": d_add, "r": reduce_second, "ar": a_route, "aret": a_return,
        "ardy": a_ready, "pre": pre, "fin": fin, "tot": total,
    }
    for op in ORDER:
        name = op.rstrip("0123456789")
        if op == "c00":
            mask(0)
        if op == "dret0":
            tab.wait()
        actions[name](*[int(c) for c in op[len(name):]])

    square = jnp.sum(acc[...])
    threshold = limit_ref[0] * math.sqrt(DW * FW)
    upper = lax.broadcasted_iota(jnp.int32, (8, 128), 0) < 4
    norm[...] = jnp.where(upper, square, threshold)
    for k in range(1, DP):
        pltpu.make_async_remote_copy(
            norm, norm_ref.at[d], n_send, n_recv,
            device_id=(lax.rem(d + k, DP), e), device_id_type=MESH,
        ).start()
    mine = pltpu.make_async_copy(norm, norm_ref.at[d], n_own)
    mine.start()

    for u in range(NU):
        pltpu.make_async_copy(
            H2.at[0, pl.ds(0, 3)], H2.at[0, pl.ds(0, 3)], y_send.at[u]
        ).wait()
    for a in range(2 * ND + 4):
        ref = d_in.at[0] if a < 2 * ND else a_in.at[0]
        pltpu.make_async_copy(
            ref.at[pl.ds(0, EX - 1)], ref.at[pl.ds(0, EX - 1)], a2a_send.at[a]
        ).wait()
    for j in range(NJ):
        out_copy(j).wait()
    mine.wait()
    three = norm_ref.at[pl.ds(0, 3)]
    pltpu.make_async_copy(three, three, n_send).wait()
    pltpu.make_async_copy(three, three, n_recv).wait()


def scale(total_ref, norm_ref, out_ref, buf, norm, in_sem, out_sem, norm_sem):
    rows = DW // DP // PARTS
    norm_in = pltpu.make_async_copy(norm_ref, norm, norm_sem)
    ins, outs = [], []
    for i in range(PARTS):
        r = pl.ds(i * rows, rows)
        ins.append(pltpu.make_async_copy(total_ref.at[r, :], buf.at[i], in_sem.at[i]))
        outs.append(pltpu.make_async_copy(buf.at[i], out_ref.at[r, :], out_sem.at[i]))
    norm_in.start()
    for copy in ins:
        copy.start()
    norm_in.wait()
    whole = norm[0] + norm[1] + norm[2] + norm[3]
    factor = jnp.minimum(1.0, norm[0, 4:5, 0:1] / jnp.sqrt(whole[0:1, 0:1] + 1e-06))
    for i in range(PARTS):
        ins[i].wait()
        buf[i] = (buf[i].astype(F32) * factor).astype(BF)
        outs[i].start()
    for copy in outs:
        copy.wait()


def local(tokens, grads_out, counts, placement, limits):
    dma = pltpu.SemaphoreType.DMA
    total, norms = pl.pallas_call(
        body,
        out_shape=(
            jax.ShapeDtypeStruct((DW // DP, FW), BF),
            jax.ShapeDtypeStruct((DP, 8, 128), F32),
        ),
        in_specs=[
            pl.BlockSpec(memory_space=pl.ANY),
            pl.BlockSpec(memory_space=pl.ANY),
            pl.BlockSpec(memory_space=pltpu.SMEM),
            pl.BlockSpec(memory_space=pltpu.VMEM),
            pl.BlockSpec(memory_space=pltpu.SMEM),
        ],
        out_specs=(
            pl.BlockSpec(memory_space=pl.ANY),
            pl.BlockSpec(memory_space=pl.ANY),
        ),
        scratch_shapes=[
            pltpu.VMEM((NX, ROWS, 4 * CH), BF),
            pltpu.VMEM((ROWS, 2 * FW), BF),
            pltpu.VMEM((NJ, 4, CH, 2 * FW), BF),
            pltpu.VMEM((2, NU, CH, HW), BF),
            pltpu.VMEM((2, NU, CH, FW), BF),
            pltpu.VMEM((ND, EX, 16, FW), BF),
            pltpu.VMEM((ND, EX, 16, FW), BF),
            pltpu.VMEM((ND, EX, 16, FW), BF),
            pltpu.VMEM((NA, CH, FW), BF),
            pltpu.VMEM((2, EX, NG, 16, 256), BF),
            pltpu.VMEM((2, EX, NG, 16, 256), BF),
            pltpu.VMEM((2, EX, NG, 16, 256), BF),
            pltpu.VMEM((EX + 1, 16, FW), F32),
            pltpu.VMEM((EX + 1, NG, 16, 256), F32),
            pltpu.VMEM((NJ, CH, FW), BF),
            pltpu.VMEM((8, FW), F32),
            pltpu.VMEM((8, 128), F32),
            pltpu.VMEM((8, 128), jnp.int32),
            pltpu.SMEM((8, 128), jnp.int32),
            pltpu.SemaphoreType.REGULAR,
            pltpu.SemaphoreType.REGULAR,
            dma((NX * 4,)),
            dma((8,)),
            dma,
            dma((NU,)),
            dma((2, NU)),
            dma((2, NU)),
            dma((2 * ND + 4,)),
            dma((2 * ND + 4,)),
            dma((2 * ND + 4,)),
            dma,
            dma,
            dma,
            dma((NJ,)),
        ],
        compiler_params=pltpu.CompilerParams(
            collective_id=0, has_side_effects=True, vmem_limit_bytes=62 * 2**20
        ),
        cost_estimate=pl.CostEstimate(
            flops=4 * ROWS * DW * FW, bytes_accessed=40 * 2**20, transcendentals=0
        ),
    )(tokens, grads_out, counts, placement.reshape(1, EX), limits)
    any_space = pl.BlockSpec(memory_space=pl.ANY)
    out = pl.pallas_call(
        scale,
        out_shape=jax.ShapeDtypeStruct((DW // DP, FW), BF),
        in_specs=[any_space, any_space],
        out_specs=any_space,
        scratch_shapes=[
            pltpu.VMEM((PARTS, DW // DP // PARTS, FW), BF),
            pltpu.VMEM((DP, 8, 128), F32),
            dma((PARTS,)),
            dma((PARTS,)),
            dma,
        ],
    )(total, norms)
    return out[None]


def solution(mesh):
    in_specs = (
        P(("dp", "expert"), None),
        P(("dp", "expert"), None),
        P(("dp", "expert"), None),
        P(),
        P("expert"),
    )
    out_specs = P("expert", "dp", None)
    return jax.shard_map(local, mesh=mesh, in_specs=in_specs, out_specs=out_specs, check_vma=False)
```

```python
import functools
import math

import jax
import jax.numpy as jnp
from jax import lax
from jax.experimental import pallas as pl
from jax.experimental.pallas import tpu as pltpu
from jax.sharding import PartitionSpec as P

MESH = pl.DeviceIdType.MESH
BF = jnp.bfloat16
F32 = jnp.float32

DP = 4
EX = 32
ROWS = 2048
DW = 3584
FW = 1024
HW = FW // 2
CH = 128
NJ = DW // DP // CH
ND = 3
NA = NJ - ND
NU = 2 * NA + ND
NG = NA // 2
NX = 3
PARTS = 4

START = ["c41", "c01"]
ORDER = [
    "c21", "w21", "h21", "c51", "dr1", "m01", "c11", "h11", "c31", "w31",
    "h31", "c00", "w00", "dret0", "h00", "m21", "c61", "m31", "c40", "dr2",
    "m00", "c30", "r0", "w11", "c10", "h10", "c20", "h20", "da0", "r3",
    "r2", "m11", "dret1", "h30", "w10", "w20", "h40", "c50", "m10", "c60",
    "dret2", "m30", "r1", "w30", "pre1", "m40", "ar0", "da1", "h50", "da2",
    "w50", "h60", "m20", "pre0", "ar1", "w60", "pre3", "aret0", "m60",
    "w40", "aret1", "m50", "ardy0", "tot4", "tot6", "pre2", "fin0", "fin1",
    "ardy1", "fin2", "fin3", "tot5",
]
STEPS = [(int(o[1]), int(o[2])) for o in START + ORDER if o[0] == "c"]


def unit(j, s):
    return j if s == 1 else NA + j


def body(
    x_ref, g_ref, counts_ref, place_ref, limit_ref, out_ref, norm_ref,
    xc, G, Pb, H1, H2, d_in, d_mid, d_back, S1, a_in, a_mid, a_back, CD, CA,
    T, acc, norm, tab_v, tab_s,
    z_sem, c_sem, x_sem, g_sem, tab_sem, y_send, h1_sem, h2_sem, a2a_send, a2a_recv, own_sem,
    n_send, n_recv, n_own, out_sem,
):
    d = lax.axis_index("dp")
    e = lax.axis_index("expert")
    up = lax.rem(d + 1, DP)
    dn = lax.rem(d + 3, DP)
    opp = lax.rem(d + 2, DP)
    ex = e // 8
    ez = lax.rem(e // 2, 4)
    ec = lax.rem(e, 2)
    turn = 1 - 2 * ec

    def peer(i):
        px = lax.rem(ex + turn * (i // 8) + 4, 4)
        pz = lax.rem(ez + turn * lax.rem(i, 4) + 4, 4)
        pc = lax.rem(ec + lax.rem(i // 4, 2), 2)
        return (px * 4 + pz) * 2 + pc

    def g_load(s, q):
        r = pl.ds(q * 512, 512)
        return pltpu.make_async_copy(
            g_ref.at[r, :], G.at[r, pl.ds(s * FW, FW)], g_sem.at[s * 4 + q]
        )

    def x_load(i, j):
        return [
            pltpu.make_async_copy(
                x_ref.at[:, pl.ds(t * (DW // DP) + j * CH, CH)],
                xc.at[i % NX, :, pl.ds(t * CH, CH)],
                x_sem.at[(i % NX) * 4 + t],
            )
            for t in range(4)
        ]

    steps = STEPS
    for q in range(4):
        g_load(1, q).start()
    for i in range(NX - 1):
        for c in x_load(i, steps[i][0]):
            c.start()
    for q in range(4):
        g_load(0, q).start()

    def at(kx, kz, kc):
        return (lax.rem(ex + kx, 4) * 4 + lax.rem(ez + kz, 4)) * 2 + lax.rem(ec + kc, 2)

    def signal(sem, td, te):
        pl.semaphore_signal(sem, inc=1, device_id=(td, te), device_id_type=MESH)

    bar = pltpu.get_barrier_semaphore()
    for k in range(1, 4):
        signal(bar, lax.rem(d + k, DP), e)
        signal(bar, d, at(k, 0, 0))
        signal(bar, d, at(0, k, 0))
    signal(bar, d, at(0, 0, 1))

    def greet_near():
        pl.semaphore_wait(bar, 10)
        for k in range(1, 4):
            signal(z_sem, d, at(0, k, 0))

    def greet_plane():
        pl.semaphore_wait(z_sem, 3)
        signal(c_sem, d, at(0, 0, 1))

    def plane_ready():
        pl.semaphore_wait(c_sem, 1)

    row = place_ref[...]
    ri = lax.broadcasted_iota(jnp.int32, (EX, EX), 0)
    ci = lax.broadcasted_iota(jnp.int32, (EX, EX), 1)
    across = jnp.broadcast_to(row, (EX, EX))
    down = jnp.sum(jnp.where(ri == ci, across, 0), axis=1, keepdims=True)
    tab_v[0:1, 0:EX] = jnp.max(
        jnp.where((down == across) & (ri < ci), ri + 1, 0), axis=0, keepdims=True
    )
    tab_v[1:2, 0:EX] = jnp.max(
        jnp.where(down == ci, ri + 1, 0), axis=0, keepdims=True
    )
    tab = pltpu.make_async_copy(tab_v, tab_s, tab_sem)
    tab.start()

    first = counts_ref[0, 0]
    second = counts_ref[0, 1]
    padded = (first + 127) // 128 * 128

    def mask(s):
        lo = padded if s == 1 else 0
        hi = padded + second if s == 1 else first
        for q in range(4):
            g_load(s, q).wait()

            @pl.loop(0, 4)
            def _(b):
                r = pl.ds(pl.multiple_of(q * 512 + b * 128, 128), 128)
                pos = lax.broadcasted_iota(jnp.int32, (128, FW), 0) + (q * 512 + b * 128)
                g = G[r, pl.ds(s * FW, FW)]
                G[r, pl.ds(s * FW, FW)] = jnp.where(
                    (pos >= lo) & (pos < hi), g, jnp.zeros_like(g)
                )

    def prefetch(n):
        if n < len(steps):
            for c in x_load(n, steps[n][0]):
                c.start()

    def product(i, start, width):
        j, s = steps[i]
        col = pl.ds(s * FW + start, width)
        r = lax.dot_general(
            xc[i % NX],
            G[:, col],
            (((0,), (0,)), ((), ())),
            preferred_element_type=F32,
        )
        Pb[j, :, :, col] = r.astype(BF).reshape(4, CH, width)

    def x_wait(i):
        for c in x_load(i, steps[i][0]):
            c.wait()

    def compute(j, s):
        i = steps.index((j, s))
        prefetch(i + NX - 1)
        x_wait(i)
        product(i, 0, FW)

    def y_copy(src, dst, u, sem, target):
        return pltpu.make_async_remote_copy(
            src, dst, y_send.at[u], sem, device_id=(target, e), device_id_type=MESH
        )

    def halves(s):
        return pl.ds(s * FW, HW), pl.ds(s * FW + HW, HW)

    left, right = pl.ds(0, HW), pl.ds(HW, HW)

    def raw_left(j, s):
        u = unit(j, s)
        ha, hb = halves(s)
        y_copy(Pb.at[j, opp, :, ha], H1.at[0, u], u, h1_sem.at[0, u], dn).start()
        y_copy(Pb.at[j, up, :, ha], H2.at[1, u, :, left], u, h2_sem.at[1, u], up).start()

    def raw_right(j, s):
        u = unit(j, s)
        ha, hb = halves(s)
        y_copy(Pb.at[j, opp, :, hb], H1.at[1, u], u, h1_sem.at[1, u], up).start()
        y_copy(Pb.at[j, dn, :, hb], H2.at[0, u, :, right], u, h2_sem.at[0, u], dn).start()

    def first_hop(j, s):
        u = unit(j, s)
        ha, hb = halves(s)
        y_copy(Pb.at[j, opp, :, ha], H1.at[0, u], u, h1_sem.at[0, u], dn).start()
        y_copy(Pb.at[j, opp, :, hb], H1.at[1, u], u, h1_sem.at[1, u], up).start()

    def whole_hop(j, s):
        u = unit(j, s)
        ha, hb = halves(s)
        y_copy(Pb.at[j, dn, :, hb], H2.at[0, u, :, right], u, h2_sem.at[0, u], dn).start()
        y_copy(Pb.at[j, up, :, ha], H2.at[1, u, :, left], u, h2_sem.at[1, u], up).start()

    def merge(j, s):
        u = unit(j, s)
        ha, hb = halves(s)
        for k, t, h, half in ((0, dn, ha, left), (1, up, hb, right)):
            pltpu.make_async_copy(H1.at[k, u], H1.at[k, u], h1_sem.at[k, u]).wait()

            @pl.loop(0, CH // 32)
            def _(b):
                r = pl.ds(pl.multiple_of(b * 32, 32), 32)
                v = Pb[j, t, r, h].astype(F32) + H1[k, u, r, :].astype(F32)
                Pb[j, t, r, h] = v.astype(BF)

            y_copy(
                Pb.at[j, t, :, h], H2.at[k, u, :, half], u, h2_sem.at[k, u], t
            ).start()

    def arrived(u):
        for k in range(2):
            pltpu.make_async_copy(H2.at[k, u], H2.at[k, u], h2_sem.at[k, u]).wait()

    def reduce_second(j):
        u = unit(j, 1)
        arrived(u)

        @pl.loop(0, CH // 16)
        def _(b):
            r = pl.ds(pl.multiple_of(b * 16, 16), 16)
            v = Pb[j, d, r, pl.ds(FW, FW)].astype(F32)
            v = v + H2[0, u, r, :].astype(F32) + H2[1, u, r, :].astype(F32)
            S1[j, r, :] = v.astype(BF)

    def one(a, src, dst, p):
        pltpu.make_async_remote_copy(
            src(p), dst.at[e], a2a_send.at[a], a2a_recv.at[a],
            device_id=(d, p), device_id_type=MESH,
        ).start()

    def keep_own(a, src, dst):
        own = pltpu.make_async_copy(src(e), dst.at[e], own_sem.at[a])
        own.start()
        return own

    def exchange(a, src, dst):
        def send(i, c):
            one(a, src, dst, peer(i))
            return c

        lax.fori_loop(1, EX, send, 0)
        return keep_own(a, src, dst)

    def all_in(a, dst):
        pltpu.make_async_copy(
            dst.at[pl.ds(0, EX - 1)], dst.at[pl.ds(0, EX - 1)], a2a_recv.at[a]
        ).wait()

    def chain(inp, mid, C):
        C[0] = jnp.zeros(C.shape[1:], F32)

        def add(i, c):
            C[i + 1] = C[tab_s[0, i]] + inp[i].astype(F32)
            return c

        lax.fori_loop(0, EX, add, 0)

        def pick(i, c):
            mid[i] = C[tab_s[1, i]].astype(BF)
            return c

        lax.fori_loop(0, EX, pick, 0)

    owns = {}

    def d_src(k, q):
        r = pl.ds(pl.multiple_of(lax.rem(q, 8) * 16, 16), 16)
        return Pb.at[NA + k, q // 8, r, pl.ds(FW, FW)]

    def d_route(k):
        owns[2 * k] = exchange(2 * k, functools.partial(d_src, k), d_in.at[k])

    def d_return(k):
        owns[2 * k].wait()
        all_in(2 * k, d_in.at[k])
        chain(d_in.at[k], d_mid.at[k], CD)
        owns[2 * k + 1] = exchange(2 * k + 1, lambda q: d_mid.at[k, q], d_back.at[k])

    def d_add(k):
        owns[2 * k + 1].wait()
        all_in(2 * k + 1, d_back.at[k])

        @pl.loop(0, EX)
        def _(q):
            t = q // 8
            r = pl.ds(pl.multiple_of(lax.rem(q, 8) * 16, 16), 16)
            v = Pb[NA + k, t, r, pl.ds(0, FW)].astype(F32) + d_back[k, q].astype(F32)
            Pb[NA + k, t, r, pl.ds(0, FW)] = v.astype(BF)

    def a_route(g):
        def src(q):
            r = pl.ds(pl.multiple_of(q // 4 * 16, 16), 16)
            c = pl.ds(pl.multiple_of(lax.rem(q, 4) * 256, 256), 256)
            return S1.at[pl.ds(g * NG, NG), r, c]

        a = 2 * (ND + g)
        owns[a] = exchange(a, src, a_in.at[g])

    def a_return(g):
        a = 2 * (ND + g)
        owns[a].wait()
        all_in(a, a_in.at[g])
        chain(a_in.at[g], a_mid.at[g], CA)
        owns[a + 1] = exchange(a + 1, lambda q: a_mid.at[g, q], a_back.at[g])

    def a_ready(g):
        a = 2 * (ND + g) + 1
        owns[a].wait()
        all_in(a, a_back.at[g])

    def sums(j, b, col):
        u = unit(j, 0)
        r = pl.ds(pl.multiple_of(b * 16, 16), 16)
        v = Pb[j, d, r, col].astype(F32)
        return v + H2[0, u, r, col].astype(F32) + H2[1, u, r, col].astype(F32)

    def finish(j, b, col, v):
        w = v * v
        acc[:, col] += w[0:8] + w[8:16]
        T[j, pl.ds(pl.multiple_of(b * 16, 16), 16), col] = v.astype(BF)

    def pre(j):
        arrived(unit(j, 0))

        @pl.loop(0, CH // 16)
        def _(b):
            CD[j * 8 + b] = sums(j, b, pl.ds(0, FW))

    def fin(j):
        @pl.loop(0, CH // 16)
        def _(b):
            for c in range(4):
                col = pl.ds(c * 256, 256)
                v = CD[j * 8 + b, :, col] + a_back[j // NG, b * 4 + c, j % NG].astype(F32)
                finish(j, b, col, v)

        out_copy(j).start()

    def total(j):
        arrived(unit(j, 0))

        @pl.loop(0, CH // 16)
        def _(b):
            for c in range(4):
                col = pl.ds(c * 256, 256)
                finish(j, b, col, sums(j, b, col))

        out_copy(j).start()

    def out_copy(j):
        return pltpu.make_async_copy(
            T.at[j], out_ref.at[pl.ds(j * CH, CH), :], out_sem.at[j]
        )

    acc[...] = jnp.zeros_like(acc)
    mask(1)
    src0 = functools.partial(d_src, 0)
    route0 = functools.partial(one, 0, src0, d_in.at[0])
    prefetch(2)
    x_wait(0)
    product(0, 0, FW)
    greet_near()
    for k in range(1, 4):
        route0(at(k, 0, 0))
        route0(at(0, k, 0))
    route0(at(0, 0, 1))
    prefetch(3)
    x_wait(1)
    product(1, 0, HW)
    raw_left(0, 1)
    greet_plane()
    for k in range(1, 4):
        for m in range(1, 4):
            route0(at(k, m, 0))
        route0(at(0, k, 1))
    product(1, HW, HW)
    raw_right(0, 1)
    plane_ready()
    for k in range(1, 4):
        for m in range(4):
            route0(at(k, m, 1))
    owns[0] = keep_own(0, src0, d_in.at[0])

    actions = {
        "c": compute, "h": first_hop, "w": whole_hop, "m": merge, "dr": d_route, "dret": d_return,
        "da": d_add, "r": reduce_second, "ar": a_route, "aret": a_return,
        "ardy": a_ready, "pre": pre, "fin": fin, "tot": total,
    }
    for op in ORDER:
        name = op.rstrip("0123456789")
        if op == "c00":
            mask(0)
        if op == "dret0":
            tab.wait()
        actions[name](*[int(c) for c in op[len(name):]])

    square = jnp.sum(acc[...])
    threshold = limit_ref[0] * math.sqrt(DW * FW)
    upper = lax.broadcasted_iota(jnp.int32, (8, 128), 0) < 4
    norm[...] = jnp.where(upper, square, threshold)
    for k in range(1, DP):
        pltpu.make_async_remote_copy(
            norm, norm_ref.at[d], n_send, n_recv,
            device_id=(lax.rem(d + k, DP), e), device_id_type=MESH,
        ).start()
    mine = pltpu.make_async_copy(norm, norm_ref.at[d], n_own)
    mine.start()

    for u in range(NU):
        pltpu.make_async_copy(
            H2.at[0, pl.ds(0, 3)], H2.at[0, pl.ds(0, 3)], y_send.at[u]
        ).wait()
    for a in range(2 * ND + 4):
        ref = d_in.at[0] if a < 2 * ND else a_in.at[0]
        pltpu.make_async_copy(
            ref.at[pl.ds(0, EX - 1)], ref.at[pl.ds(0, EX - 1)], a2a_send.at[a]
        ).wait()
    for j in range(NJ):
        out_copy(j).wait()
    mine.wait()
    three = norm_ref.at[pl.ds(0, 3)]
    pltpu.make_async_copy(three, three, n_send).wait()
    pltpu.make_async_copy(three, three, n_recv).wait()


def scale(total_ref, norm_ref, out_ref, buf, norm, in_sem, out_sem, norm_sem):
    rows = DW // DP // PARTS
    norm_in = pltpu.make_async_copy(norm_ref, norm, norm_sem)
    ins, outs = [], []
    for i in range(PARTS):
        r = pl.ds(i * rows, rows)
        ins.append(pltpu.make_async_copy(total_ref.at[r, :], buf.at[i], in_sem.at[i]))
        outs.append(pltpu.make_async_copy(buf.at[i], out_ref.at[r, :], out_sem.at[i]))
    norm_in.start()
    for copy in ins:
        copy.start()
    norm_in.wait()
    whole = norm[0] + norm[1] + norm[2] + norm[3]
    factor = jnp.minimum(1.0, norm[0, 4:5, 0:1] / jnp.sqrt(whole[0:1, 0:1] + 1e-06))
    for i in range(PARTS):
        ins[i].wait()
        buf[i] = (buf[i].astype(F32) * factor).astype(BF)
        outs[i].start()
    for copy in outs:
        copy.wait()


def local(tokens, grads_out, counts, placement, limits):
    dma = pltpu.SemaphoreType.DMA
    total, norms = pl.pallas_call(
        body,
        out_shape=(
            jax.ShapeDtypeStruct((DW // DP, FW), BF),
            jax.ShapeDtypeStruct((DP, 8, 128), F32),
        ),
        in_specs=[
            pl.BlockSpec(memory_space=pl.ANY),
            pl.BlockSpec(memory_space=pl.ANY),
            pl.BlockSpec(memory_space=pltpu.SMEM),
            pl.BlockSpec(memory_space=pltpu.VMEM),
            pl.BlockSpec(memory_space=pltpu.SMEM),
        ],
        out_specs=(
            pl.BlockSpec(memory_space=pl.ANY),
            pl.BlockSpec(memory_space=pl.ANY),
        ),
        scratch_shapes=[
            pltpu.VMEM((NX, ROWS, 4 * CH), BF),
            pltpu.VMEM((ROWS, 2 * FW), BF),
            pltpu.VMEM((NJ, 4, CH, 2 * FW), BF),
            pltpu.VMEM((2, NU, CH, HW), BF),
            pltpu.VMEM((2, NU, CH, FW), BF),
            pltpu.VMEM((ND, EX, 16, FW), BF),
            pltpu.VMEM((ND, EX, 16, FW), BF),
            pltpu.VMEM((ND, EX, 16, FW), BF),
            pltpu.VMEM((NA, CH, FW), BF),
            pltpu.VMEM((2, EX, NG, 16, 256), BF),
            pltpu.VMEM((2, EX, NG, 16, 256), BF),
            pltpu.VMEM((2, EX, NG, 16, 256), BF),
            pltpu.VMEM((EX + 1, 16, FW), F32),
            pltpu.VMEM((EX + 1, NG, 16, 256), F32),
            pltpu.VMEM((NJ, CH, FW), BF),
            pltpu.VMEM((8, FW), F32),
            pltpu.VMEM((8, 128), F32),
            pltpu.VMEM((8, 128), jnp.int32),
            pltpu.SMEM((8, 128), jnp.int32),
            pltpu.SemaphoreType.REGULAR,
            pltpu.SemaphoreType.REGULAR,
            dma((NX * 4,)),
            dma((8,)),
            dma,
            dma((NU,)),
            dma((2, NU)),
            dma((2, NU)),
            dma((2 * ND + 4,)),
            dma((2 * ND + 4,)),
            dma((2 * ND + 4,)),
            dma,
            dma,
            dma,
            dma((NJ,)),
        ],
        compiler_params=pltpu.CompilerParams(
            collective_id=0, has_side_effects=True, vmem_limit_bytes=62 * 2**20
        ),
        cost_estimate=pl.CostEstimate(
            flops=4 * ROWS * DW * FW, bytes_accessed=40 * 2**20, transcendentals=0
        ),
    )(tokens, grads_out, counts, placement.reshape(1, EX), limits)
    any_space = pl.BlockSpec(memory_space=pl.ANY)
    out = pl.pallas_call(
        scale,
        out_shape=jax.ShapeDtypeStruct((DW // DP, FW), BF),
        in_specs=[any_space, any_space],
        out_specs=any_space,
        scratch_shapes=[
            pltpu.VMEM((PARTS, DW // DP // PARTS, FW), BF),
            pltpu.VMEM((DP, 8, 128), F32),
            dma((PARTS,)),
            dma((PARTS,)),
            dma,
        ],
    )(total, norms)
    return out[None]


def solution(mesh):
    in_specs = (
        P(("dp", "expert"), None),
        P(("dp", "expert"), None),
        P(("dp", "expert"), None),
        P(),
        P("expert"),
    )
    out_specs = P("expert", "dp", None)
    return jax.shard_map(local, mesh=mesh, in_specs=in_specs, out_specs=out_specs, check_vma=False)
```
